256 devices in a mesh: rep: 4 (over z_lo), fsdp: 64 (over z_hi, x, y, core).
Axes of the slice: x: 4, y: 4, z: 8 (z_hi: 2, z_lo: 4; z = z_hi * 4 + z_lo), core: 2. Of those that a mesh axis runs over, the one named last changes fastest.
Arguments:
- activations: bfloat16 [1, 32768, 4096], P(None, ('rep', 'fsdp')), may hold values from -24 to 24
- unit_grads: bfloat16 [1, 32768, 11008], P(None, ('rep', 'fsdp')), may hold values from -0.0625 to 0.0625
- momentum: float32 [4, 1, 4096, 11008], P('rep', None, 'fsdp'), may hold values from -6 to 6
Outputs:
- update: float32 [1, 4096, 11008], P(None, 'fsdp')
- new_momentum: float32 [4, 1, 4096, 11008], P('rep', None, 'fsdp')
The draws below stay inside these ranges and needn't reach their ends.
All inputs are finite; a program needn't handle non-finite values.
Results may differ from the reference program's by a relative error of at most 0.0003.
Values may be sent and summed in bfloat16 or wider, within the bound.
No kernel may reach another device: no remote copies, remote signals or barrier semaphores. Data moves between devices by JAX's collectives and lax.ppermute only.
A program may use at most 192 MiB of HBM per device.

```python
import jax
import jax.numpy as jnp
from jax import lax

D = 4096
R = 11008
LAYERS = 1
SPAN = 64
BAND = 8
TOK_DEV = 128
TOKENS = 32768
N_REP = 4
N_FSDP = 64


def spiked(result, key, source, target, shards_of, factor):
    def block_of(position):
        return (jnp.arange(result.shape[position]) // (result.shape[position] // shards_of)).reshape((-1,) + (1,) * (result.ndim - 1 - position))

    one_side = jax.random.permutation(key, shards_of)[block_of(target)]
    second = (block_of(target) + shards_of // 2) % shards_of
    return jnp.where((block_of(source) == one_side) | (block_of(source) == second), factor * result, result)


def block_levels(rng, dims, pieces, smallest, top_value):
    def one(position, blocks):
        heights = jax.random.uniform(jax.random.fold_in(jax.random.fold_in(rng, 6), position), (blocks,), jnp.float32, smallest / len(pieces), top_value / len(pieces))
        return jnp.repeat(jnp.exp(heights), dims[position] // blocks).reshape((-1,) + (1,) * (len(dims) - position - 1))

    factor_of = one(*pieces[0])
    for cut in pieces[1:]:
        factor_of = factor_of * one(*cut)
    return factor_of


def bell_draw(rng, shape, spread, reach, split=(), kind=jnp.bfloat16):
    array = spread * jax.random.normal(rng, shape, jnp.float32)
    if split:
        array = array * block_levels(rng, shape, split, -0.22, 0.18)
    return jnp.clip(array, -reach, reach).astype(kind)


def heavy_noise(stream_key, dims, deviation, reach, cuts, heavy, kind=jnp.bfloat16):
    result = deviation * jax.random.normal(stream_key, dims, jnp.float32)
    if cuts:
        result = result * block_levels(stream_key, dims, cuts, -0.22, 0.18)
    return jnp.clip(spiked(result, jax.random.fold_in(stream_key, 3), *heavy), -reach, reach).astype(kind)


def setup_inputs(seed: int = 0) -> dict:
    arg_keys = jax.random.split(jax.random.key(seed), 4)
    activations = heavy_noise(arg_keys[0], (LAYERS, TOKENS, D), 1.0, 24.0, ((1, 256),), (1, 2, 256, 6.0))
    unit_grads = bell_draw(arg_keys[1], (LAYERS, TOKENS, R), (TOK_DEV * N_FSDP) ** -0.5, 0.0625, ((1, 256),))
    momentum = bell_draw(arg_keys[2], (N_REP, LAYERS, D, R), 1.0, 6.0, ((0, 4), (2, 64)), jnp.float32)
    return dict(activations=activations, unit_grads=unit_grads, momentum=momentum)


decay_rate = 0.9

def band_table():
    freqs = jnp.arange(BAND, dtype=jnp.float32)[:, None]
    points = jnp.arange(SPAN, dtype=jnp.float32)[None, :]
    scales = jnp.where(freqs == 0.0, jnp.sqrt(1.0 / SPAN), jnp.sqrt(2.0 / SPAN))
    return scales * jnp.cos(jnp.pi * (2.0 * points + 1.0) * freqs / (2.0 * SPAN))

def to_band(matrix, basis):
    rows, cols = matrix.shape
    blocks = matrix.reshape(rows // SPAN, SPAN, cols // SPAN, SPAN)
    return jnp.einsum('kb,abcd,jd->akcj', basis, blocks, basis, precision=lax.Precision.HIGHEST)

def from_band(band, basis):
    blocks = jnp.einsum('kb,akcj,jd->abcd', basis, band, basis, precision=lax.Precision.HIGHEST)
    return blocks.reshape(band.shape[0] * SPAN, band.shape[2] * SPAN)

def reference(activations, unit_grads, momentum):
    basis = band_table()
    group_rows = TOK_DEV * N_FSDP
    layer_updates = []
    group_moms = [[] for group in range(N_REP)]
    for layer in range(LAYERS):
        total = None
        for group in range(N_REP):
            lower = group * group_rows
            grads = jnp.dot(activations[layer, lower:lower + group_rows].T, unit_grads[layer, lower:lower + group_rows], preferred_element_type=jnp.float32)
            mixed = decay_rate * momentum[group, layer] + grads
            band = to_band(mixed, basis)
            group_moms[group].append(mixed - from_band(band, basis))
            total = band if total is None else total + band
        layer_updates.append(from_band(total, basis) / N_REP)
    update = jnp.stack(layer_updates)
    new_momentum = jnp.stack([jnp.stack(group_moms[group]) for group in range(N_REP)])
    return (update, new_momentum)
```

```python
import functools

import jax
import jax.numpy as jnp
import numpy as np
from jax import lax
from jax.experimental import pallas as pl
from jax.experimental.pallas import tpu as pltpu
from jax.sharding import Mesh
from jax.sharding import PartitionSpec as P

SPAN = 64
BAND = 8
LANES = 128
GROUP = 1024
DECAY = 0.9
CHUNK_TILES = (4, 4, 3)
PARAMS = pltpu.CompilerParams(vmem_limit_bytes=56 << 20)
ANY = pl.BlockSpec(memory_space=pl.ANY)
QUICK = pl.CostEstimate(flops=1, bytes_accessed=1, transcendentals=0)
SMEM = pl.BlockSpec(memory_space=pltpu.SMEM)
VMEM = pl.BlockSpec(memory_space=pltpu.VMEM)


def band_table():
    freqs = np.arange(BAND, dtype=np.float64)[:, None]
    points = np.arange(SPAN, dtype=np.float64)[None, :]
    scales = np.where(freqs == 0.0, np.sqrt(1.0 / SPAN), np.sqrt(2.0 / SPAN))
    return (scales * np.cos(np.pi * (2.0 * points + 1.0) * freqs / (2.0 * SPAN))).astype(np.float32)


def shift(n, by):
    return [(i, (i + by) % n) for i in range(n)]


def halved(value):
    high = value.astype(jnp.bfloat16)
    return high, (value - high.astype(jnp.float32)).astype(jnp.bfloat16)


def dot(a, b):
    (ah, al), (bh, bl) = halved(a), halved(b)
    return jnp.dot(
        jnp.concatenate([ah, ah, al], axis=1),
        jnp.concatenate([bh, bl, bh], axis=0),
        preferred_element_type=jnp.float32,
    )


def groups_of(width):
    return [(start, min(GROUP, width - start)) for start in range(0, width, GROUP)]


def starts_of(width, block):
    return [min(j * block, width - block) for j in range(8)]


def finish_kernel(widths, basis_ref, back_ref, wide_ref, tall_ref, mom_ref, *refs):
    n = len(widths)
    pieces, (new_ref, band_ref, rows_ref) = refs[:n], refs[n:]
    width = mom_ref.shape[1]
    for j, start in enumerate(starts_of(width, sum(widths))):
        for k, w in enumerate(widths):
            at = pl.ds(start + sum(widths[:k]), w)
            new_ref[:, at] = DECAY * mom_ref[:, at] + pieces[k][j]
    rows_ref[...] = jnp.zeros_like(rows_ref)
    for i, (start, w) in enumerate(groups_of(width)):
        rows_ref[i * BAND : (i + 1) * BAND, :w] = dot(basis_ref[...], new_ref[:, start : start + w])
    band = dot(rows_ref[...], wide_ref[...])
    band_ref[...] = band
    rows_ref[...] = dot(band, tall_ref[...])
    for i, (start, w) in enumerate(groups_of(width)):
        new_ref[:, start : start + w] -= dot(back_ref[...], rows_ref[i * BAND : (i + 1) * BAND, :w])


def update_kernel(back_ref, tall_ref, b0, b1, b2, b3, out_ref):
    total = ((b0[...] + b1[...]) + (b2[...] + b3[...])) * 0.25
    rows = dot(total, tall_ref[...])
    for i, (start, w) in enumerate(groups_of(out_ref.shape[1])):
        out_ref[:, start : start + w] = dot(back_ref[...], rows[i * BAND : (i + 1) * BAND, :w])


def call(kernel, out, *args, spec=None):
    shapes = [jax.ShapeDtypeStruct(s, t) for s, t in out]
    return pl.pallas_call(
        kernel,
        out_shape=shapes,
        in_specs=spec or [VMEM] * len(args),
        out_specs=[VMEM] * len(out),
        compiler_params=PARAMS,
        cost_estimate=QUICK,
    )(*args)


def strips_kernel(half, at_ref, acts_ref, *outs):
    for e, out in enumerate(outs):
        for i in range(2):
            at = pl.ds(pl.multiple_of(at_ref[2 * e + i], LANES), half)
            out[i * half : (i + 1) * half] = acts_ref[:, at].T


def blocks_kernel(starts, leads, units_ref, *outs):
    for lead, out in zip(leads, outs):
        for j, start in enumerate(starts):
            out[j] = units_ref[:, start + lead : start + lead + out.shape[2]]


def blocks(units, starts, leads, widths):
    outs = [((8, units.shape[0], w), units.dtype) for w in widths]
    return call(functools.partial(blocks_kernel, starts, leads), outs, units)


def product(left, rights):
    total = None
    for i, some in enumerate(((0,), (1,), (2,), (3, 4))):
        count = 8 // len(some)
        for m, n in enumerate(some):
            part = jnp.concatenate([left[count * m + j, i] for j in range(count)], axis=1)
            term = jnp.dot(part, rights[n][...], preferred_element_type=jnp.float32)
            total = term if total is None else total + term
    return total


def keep_kernel(left_ref, *refs):
    refs[5][...] = product(left_ref, refs[:5])


def send_kernel(left_ref, *refs):
    rights, out, top_ref = refs[:5], refs[5], refs[6]
    i, rows = pl.program_id(0), left_ref.shape[2]
    value = product(left_ref, rights)
    top = jnp.max(jnp.max(jnp.abs(value), axis=0, keepdims=True), axis=1, keepdims=True)

    @pl.when(i == 0)
    def _():
        top_ref[...] = jnp.zeros_like(top_ref)

    top_ref[...] = jnp.maximum(top_ref[...], top)
    out[pl.ds(pl.multiple_of(i * rows, rows), rows)] = value

    @pl.when(i == pl.num_programs(0) - 1)
    def _():
        half, w = out.shape[0] - 16, out.shape[1]
        power = jnp.floor(15.0 - jnp.log2(jnp.maximum(top_ref[:1, :1], 2.0**-100)))
        out[:half] = out[:half] * jnp.exp2(power)
        out[half:] = jnp.broadcast_to(power, (16, w))


def tile(kernel, lefts, rights, extra):
    n, dx, half, tok = lefts.shape
    w = rights[0].shape[1]
    rows = 256
    if extra:
        out_spec = pl.BlockSpec((half + extra, w), lambda i: (0, 0))
        scratch = [pltpu.VMEM((8, LANES), jnp.float32)]
    else:
        out_spec = pl.BlockSpec((rows, w), lambda i: (i, 0))
        scratch = []
    in_specs = [pl.BlockSpec((n, dx, rows, tok), lambda i: (0, 0, i, 0))]
    depth = rights[0].shape[0]
    for n, b in enumerate(rights):
        size = depth if n < 3 else depth // 2
        place = 0 if n < 3 else b.shape[0] // size - 1
        in_specs.append(pl.BlockSpec((size, w), lambda i, place=place: (place, 0)))
    return pl.pallas_call(
        kernel,
        grid=(half // rows,),
        out_shape=jax.ShapeDtypeStruct((half + extra, w), jnp.float32),
        in_specs=in_specs,
        out_specs=out_spec,
        scratch_shapes=scratch,
        compiler_params=PARAMS,
        cost_estimate=QUICK,
    )(lefts, *rights)


def on_device(activations, unit_grads, momentum):
    acts, units, mom = activations[0], unit_grads[0], momentum[0, 0]
    tok, features = acts.shape
    width = units.shape[1]
    zh, x = lax.axis_index("zh"), lax.axis_index("x")
    plane_rows = features // 2
    half = plane_rows // 4
    own_rows = half // 8
    block = -(-width // (8 * LANES)) * LANES
    widths = [LANES * t for t in CHUNK_TILES]
    f32, b16 = jnp.float32, acts.dtype

    def along(axis, by, value):
        return lax.ppermute(value, axis, shift(2 if axis in ("core", "zh") else 4, by))

    def sync(*values):
        return lax.optimization_barrier(values)

    def swap(value):
        return lax.all_to_all(value, ("y", "core"), 0, 0, tiled=True)

    def column_block(cut):
        return swap(cut).reshape(8 * tok, cut.shape[2])

    def ring(v):
        return along("x", 1, v), along("x", 3, v)

    def halves(r, l):
        depth = 4 * tok
        return r[:depth], l[depth : 2 * depth]

    def payload(sent, five):
        return tile(send_kernel, sent, five, 16).astype(jnp.float16)

    def joined(keep, got):
        other = got[:half].astype(f32) * jnp.exp2(-got[half : half + 1].astype(f32))
        return (keep + other).reshape(8, own_rows, keep.shape[1])

    strips_at = jnp.stack(
        [plane_rows * p + half * ((x + e) % 4) for e in range(4) for p in (zh, 1 - zh)]
    ).astype(jnp.int32)

    starts = starts_of(width, block)
    leads = [sum(widths[:k]) for k in range(len(widths))]

    (cut0,) = blocks(units, starts, leads[:1], widths[:1])
    v0 = column_block(cut0)
    s0, s1, s2, s3 = call(
        functools.partial(strips_kernel, half), [((2 * half, tok), b16)] * 4, strips_at, acts, spec=[SMEM, VMEM]
    )
    local = [s0, along("x", 1, s1), along("x", 3, s3), along("x", 2, s2)]
    kept = jnp.stack([a[:half] for a in local])
    sent = jnp.stack([a[half:] for a in local])

    v0, sent, units = sync(v0, sent, units)
    r0, l0 = ring(v0)
    cut1, cut2 = blocks(units, starts, leads[1:], widths[1:])
    v1 = column_block(cut1)

    v1, r0, l0, sent, kept, cut2 = sync(v1, r0, l0, sent, kept, cut2)
    far_r, far_l = halves(r0, l0)
    right, left = jnp.concatenate([v1, far_r]), jnp.concatenate([v1, far_l])
    right, left, sent, kept, cut2 = sync(right, left, sent, kept, cut2)
    r1, l1 = along("x", 1, right), along("x", 3, left)
    v2 = column_block(cut2)
    sent = lax.all_gather(sent, ("y", "core"))

    r1, l1, v2, sent, kept = sync(r1, l1, v2, sent, kept)
    half1 = halves(r1, l1)
    half1, r1, l1, v2, sent, kept = sync(half1, r1, l1, v2, sent, kept)
    far1 = along("x", 1, half1[0]), along("x", 3, half1[1])
    send0 = payload(sent, [v0, r0, l0, r1, l1])
    kept = lax.all_gather(kept, ("y", "core"))

    far1, send0, v2, sent = sync(far1, send0, v2, sent)
    r2, l2 = ring(v2)
    got0 = along("zh", 1, send0)
    send1 = payload(sent, [v1, r1, l1, *far1])

    r2, l2, got0, send1, kept = sync(r2, l2, got0, send1, kept)
    half2 = halves(r2, l2)
    half2, got0, send1, kept = sync(half2, got0, send1, kept)
    far2 = along("x", 1, half2[0]), along("x", 3, half2[1])
    got1 = along("zh", 1, send1)
    send2 = payload(sent, [v2, r2, l2, *far2])
    total0 = joined(tile(keep_kernel, kept, [v0, r0, l0, r1, l1], 0), got0)

    got1, send2, total0, kept = sync(got1, send2, total0, kept)
    got2 = along("zh", 1, send2)
    done0 = swap(total0)
    total1 = joined(tile(keep_kernel, kept, [v1, r1, l1, *far1], 0), got1)
    keep2 = tile(keep_kernel, kept, [v2, r2, l2, *far2], 0)

    got2, done0, total1, keep2 = sync(got2, done0, total1, keep2)
    done = [done0, swap(total1), swap(joined(keep2, got2))]

    basis = band_table()
    wide = np.kron(np.eye(GROUP // SPAN, dtype=np.float32), basis.T)
    rows = len(groups_of(width)) * BAND
    with jax.named_scope("finish"):
        new, band = pl.pallas_call(
            functools.partial(finish_kernel, widths),
            out_shape=(
                jax.ShapeDtypeStruct(mom.shape, f32),
                jax.ShapeDtypeStruct((rows, LANES), f32),
            ),
            in_specs=[VMEM] * (5 + len(widths)),
            out_specs=(VMEM, VMEM),
            scratch_shapes=[pltpu.VMEM((rows, GROUP), f32)],
            compiler_params=PARAMS,
        )(basis, basis.T, wide, wide.T, mom, *done)
    with jax.named_scope("band"):
        others = [along("rep", s, band) for s in (1, 2, 3)]
    with jax.named_scope("update"):
        (update,) = call(update_kernel, [(mom.shape, f32)], jnp.asarray(basis.T), jnp.asarray(wide.T), band, *others)
    return update[None], new[None, None]


def solution(mesh):
    fine = Mesh(mesh.devices.reshape(4, 2, 4, 4, 2), ("rep", "zh", "x", "y", "core"))
    every = ("rep", "zh", "x", "y", "core")
    return jax.shard_map(
        on_device,
        mesh=fine,
        in_specs=(
            P(None, every, None),
            P(None, every, None),
            P("rep", None, every[1:], None),
        ),
        out_specs=(P(None, every[1:], None), P("rep", None, every[1:], None)),
        check_vma=False,
    )
```

```python
import functools

import jax
import jax.numpy as jnp
import numpy as np
from jax import lax
from jax.experimental import pallas as pl
from jax.experimental.pallas import tpu as pltpu
from jax.sharding import Mesh
from jax.sharding import PartitionSpec as P

SPAN = 64
BAND = 8
LANES = 128
GROUP = 1024
DECAY = 0.9
CHUNK_TILES = (4, 4, 3)
PARAMS = pltpu.CompilerParams(vmem_limit_bytes=56 << 20)
ANY = pl.BlockSpec(memory_space=pl.ANY)
QUICK = pl.CostEstimate(flops=1, bytes_accessed=1, transcendentals=0)
SMEM = pl.BlockSpec(memory_space=pltpu.SMEM)
VMEM = pl.BlockSpec(memory_space=pltpu.VMEM)


def band_table():
    freqs = np.arange(BAND, dtype=np.float64)[:, None]
    points = np.arange(SPAN, dtype=np.float64)[None, :]
    scales = np.where(freqs == 0.0, np.sqrt(1.0 / SPAN), np.sqrt(2.0 / SPAN))
    return (scales * np.cos(np.pi * (2.0 * points + 1.0) * freqs / (2.0 * SPAN))).astype(np.float32)


def shift(n, by):
    return [(i, (i + by) % n) for i in range(n)]


def halved(value):
    high = value.astype(jnp.bfloat16)
    return high, (value - high.astype(jnp.float32)).astype(jnp.bfloat16)


def dot(a, b):
    (ah, al), (bh, bl) = halved(a), halved(b)
    return jnp.dot(
        jnp.concatenate([ah, ah, al], axis=1),
        jnp.concatenate([bh, bl, bh], axis=0),
        preferred_element_type=jnp.float32,
    )


def groups_of(width):
    return [(start, min(GROUP, width - start)) for start in range(0, width, GROUP)]


def starts_of(width, block):
    return [min(j * block, width - block) for j in range(8)]


def finish_kernel(widths, basis_ref, back_ref, wide_ref, tall_ref, mom_ref, *refs):
    n = len(widths)
    pieces, (new_ref, band_ref, rows_ref) = refs[:n], refs[n:]
    width = mom_ref.shape[1]
    for j, start in enumerate(starts_of(width, sum(widths))):
        for k, w in enumerate(widths):
            at = pl.ds(start + sum(widths[:k]), w)
            new_ref[:, at] = DECAY * mom_ref[:, at] + pieces[k][j]
    rows_ref[...] = jnp.zeros_like(rows_ref)
    for i, (start, w) in enumerate(groups_of(width)):
        rows_ref[i * BAND : (i + 1) * BAND, :w] = dot(basis_ref[...], new_ref[:, start : start + w])
    band = dot(rows_ref[...], wide_ref[...])
    band_ref[...] = band
    rows_ref[...] = dot(band, tall_ref[...])
    for i, (start, w) in enumerate(groups_of(width)):
        new_ref[:, start : start + w] -= dot(back_ref[...], rows_ref[i * BAND : (i + 1) * BAND, :w])


def update_kernel(back_ref, tall_ref, b0, b1, b2, b3, out_ref):
    total = ((b0[...] + b1[...]) + (b2[...] + b3[...])) * 0.25
    rows = dot(total, tall_ref[...])
    for i, (start, w) in enumerate(groups_of(out_ref.shape[1])):
        out_ref[:, start : start + w] = dot(back_ref[...], rows[i * BAND : (i + 1) * BAND, :w])


def call(kernel, out, *args, spec=None):
    shapes = [jax.ShapeDtypeStruct(s, t) for s, t in out]
    return pl.pallas_call(
        kernel,
        out_shape=shapes,
        in_specs=spec or [VMEM] * len(args),
        out_specs=[VMEM] * len(out),
        compiler_params=PARAMS,
        cost_estimate=QUICK,
    )(*args)


def strips_kernel(half, at_ref, acts_ref, *outs):
    for e, out in enumerate(outs):
        for i in range(2):
            at = pl.ds(pl.multiple_of(at_ref[2 * e + i], LANES), half)
            out[i * half : (i + 1) * half] = acts_ref[:, at].T


def blocks_kernel(starts, leads, units_ref, *outs):
    for lead, out in zip(leads, outs):
        for j, start in enumerate(starts):
            out[j] = units_ref[:, start + lead : start + lead + out.shape[2]]


def blocks(units, starts, leads, widths):
    outs = [((8, units.shape[0], w), units.dtype) for w in widths]
    return call(functools.partial(blocks_kernel, starts, leads), outs, units)


def product(left, rights):
    total = None
    for i, some in enumerate(((0,), (1,), (2,), (3, 4))):
        count = 8 // len(some)
        for m, n in enumerate(some):
            part = jnp.concatenate([left[count * m + j, i] for j in range(count)], axis=1)
            term = jnp.dot(part, rights[n][...], preferred_element_type=jnp.float32)
            total = term if total is None else total + term
    return total


def keep_kernel(left_ref, *refs):
    refs[5][...] = product(left_ref, refs[:5])


def send_kernel(left_ref, *refs):
    rights, out, top_ref = refs[:5], refs[5], refs[6]
    i, rows = pl.program_id(0), left_ref.shape[2]
    value = product(left_ref, rights)
    top = jnp.max(jnp.max(jnp.abs(value), axis=0, keepdims=True), axis=1, keepdims=True)

    @pl.when(i == 0)
    def _():
        top_ref[...] = jnp.zeros_like(top_ref)

    top_ref[...] = jnp.maximum(top_ref[...], top)
    out[pl.ds(pl.multiple_of(i * rows, rows), rows)] = value

    @pl.when(i == pl.num_programs(0) - 1)
    def _():
        half, w = out.shape[0] - 16, out.shape[1]
        power = jnp.floor(15.0 - jnp.log2(jnp.maximum(top_ref[:1, :1], 2.0**-100)))
        out[:half] = out[:half] * jnp.exp2(power)
        out[half:] = jnp.broadcast_to(power, (16, w))


def tile(kernel, lefts, rights, extra):
    n, dx, half, tok = lefts.shape
    w = rights[0].shape[1]
    rows = 256
    if extra:
        out_spec = pl.BlockSpec((half + extra, w), lambda i: (0, 0))
        scratch = [pltpu.VMEM((8, LANES), jnp.float32)]
    else:
        out_spec = pl.BlockSpec((rows, w), lambda i: (i, 0))
        scratch = []
    in_specs = [pl.BlockSpec((n, dx, rows, tok), lambda i: (0, 0, i, 0))]
    depth = rights[0].shape[0]
    for n, b in enumerate(rights):
        size = depth if n < 3 else depth // 2
        place = 0 if n < 3 else b.shape[0] // size - 1
        in_specs.append(pl.BlockSpec((size, w), lambda i, place=place: (place, 0)))
    return pl.pallas_call(
        kernel,
        grid=(half // rows,),
        out_shape=jax.ShapeDtypeStruct((half + extra, w), jnp.float32),
        in_specs=in_specs,
        out_specs=out_spec,
        scratch_shapes=scratch,
        compiler_params=PARAMS,
        cost_estimate=QUICK,
    )(lefts, *rights)


def join_kernel(*refs):
    out, lead = refs[-1], 0
    for keep_ref, got_ref in zip(refs[:-1:2], refs[1:-1:2]):
        half, w = keep_ref.shape
        scale = jnp.exp2(-got_ref[half : half + 1, :1])
        out[:, lead : lead + w] = keep_ref[...] + got_ref[:half] * scale
        lead += w


def on_device(activations, unit_grads, momentum):
    acts, units, mom = activations[0], unit_grads[0], momentum[0, 0]
    tok, features = acts.shape
    width = units.shape[1]
    zh, x = lax.axis_index("zh"), lax.axis_index("x")
    plane_rows = features // 2
    half = plane_rows // 4
    own_rows = half // 8
    block = -(-width // (8 * LANES)) * LANES
    widths = [LANES * t for t in CHUNK_TILES]
    f32, b16 = jnp.float32, acts.dtype

    def along(axis, by, value):
        return lax.ppermute(value, axis, shift(2 if axis in ("core", "zh") else 4, by))

    def sync(*values):
        return lax.optimization_barrier(values)

    def swap(value):
        return lax.all_to_all(value, ("y", "core"), 0, 0, tiled=True)

    def column_block(cut):
        return swap(cut).reshape(8 * tok, cut.shape[2])

    def ring(v):
        return along("x", 1, v), along("x", 3, v)

    def halves(r, l):
        depth = 4 * tok
        return r[:depth], l[depth : 2 * depth]

    def payload(sent, five):
        return tile(send_kernel, sent, five, 16).astype(jnp.float16)

    def joined(keep, got):
        other = got[:half].astype(f32) * jnp.exp2(-got[half : half + 1].astype(f32))
        return (keep + other).reshape(8, own_rows, keep.shape[1])

    strips_at = jnp.stack(
        [plane_rows * p + half * ((x + e) % 4) for e in range(4) for p in (zh, 1 - zh)]
    ).astype(jnp.int32)

    starts = starts_of(width, block)
    leads = [sum(widths[:k]) for k in range(len(widths))]

    (cut0,) = blocks(units, starts, leads[:1], widths[:1])
    v0 = column_block(cut0)
    s0, s1, s2, s3 = call(
        functools.partial(strips_kernel, half), [((2 * half, tok), b16)] * 4, strips_at, acts, spec=[SMEM, VMEM]
    )
    local = [s0, along("x", 1, s1), along("x", 3, s3), along("x", 2, s2)]
    kept = jnp.stack([a[:half] for a in local])
    sent = jnp.stack([a[half:] for a in local])

    v0, sent, units = sync(v0, sent, units)
    r0, l0 = ring(v0)
    cut1, cut2 = blocks(units, starts, leads[1:], widths[1:])
    v1 = column_block(cut1)

    v1, r0, l0, sent, kept, cut2 = sync(v1, r0, l0, sent, kept, cut2)
    far_r, far_l = halves(r0, l0)
    right, left = jnp.concatenate([v1, far_r]), jnp.concatenate([v1, far_l])
    right, left, sent, kept, cut2 = sync(right, left, sent, kept, cut2)
    r1, l1 = along("x", 1, right), along("x", 3, left)
    v2 = column_block(cut2)
    sent = lax.all_gather(sent, ("y", "core"))

    r1, l1, v2, sent, kept = sync(r1, l1, v2, sent, kept)
    half1 = halves(r1, l1)
    half1, r1, l1, v2, sent, kept = sync(half1, r1, l1, v2, sent, kept)
    far1 = along("x", 1, half1[0]), along("x", 3, half1[1])
    send0 = payload(sent, [v0, r0, l0, r1, l1])
    kept = lax.all_gather(kept, ("y", "core"))

    far1, send0, v2, sent = sync(far1, send0, v2, sent)
    r2, l2 = ring(v2)
    got0 = along("zh", 1, send0)
    send1 = payload(sent, [v1, r1, l1, *far1])

    r2, l2, got0, send1, kept = sync(r2, l2, got0, send1, kept)
    half2 = halves(r2, l2)
    half2, got0, send1, kept = sync(half2, got0, send1, kept)
    far2 = along("x", 1, half2[0]), along("x", 3, half2[1])
    got1 = along("zh", 1, send1)
    send2 = payload(sent, [v2, r2, l2, *far2])
    total0 = joined(tile(keep_kernel, kept, [v0, r0, l0, r1, l1], 0), got0)

    got1, send2, total0, kept = sync(got1, send2, total0, kept)
    got2 = along("zh", 1, send2)
    done0 = swap(total0)
    keep1 = tile(keep_kernel, kept, [v1, r1, l1, *far1], 0)
    keep2 = tile(keep_kernel, kept, [v2, r2, l2, *far2], 0)
    other1 = got1.astype(f32)

    got2, done0, keep1, keep2, other1 = sync(got2, done0, keep1, keep2, other1)
    late = block - widths[0]
    (total,) = call(join_kernel, [((half, late), f32)], keep1, other1, keep2, got2.astype(f32))
    done = [done0, swap(total.reshape(8, own_rows, late))]

    basis = band_table()
    wide = np.kron(np.eye(GROUP // SPAN, dtype=np.float32), basis.T)
    rows = len(groups_of(width)) * BAND
    with jax.named_scope("finish"):
        new, band = pl.pallas_call(
            functools.partial(finish_kernel, [d.shape[2] for d in done]),
            out_shape=(
                jax.ShapeDtypeStruct(mom.shape, f32),
                jax.ShapeDtypeStruct((rows, LANES), f32),
            ),
            in_specs=[VMEM] * (5 + len(done)),
            out_specs=(VMEM, VMEM),
            scratch_shapes=[pltpu.VMEM((rows, GROUP), f32)],
            compiler_params=PARAMS,
        )(basis, basis.T, wide, wide.T, mom, *done)
    with jax.named_scope("band"):
        others = [along("rep", s, band) for s in (1, 2, 3)]
    with jax.named_scope("update"):
        (update,) = call(update_kernel, [(mom.shape, f32)], jnp.asarray(basis.T), jnp.asarray(wide.T), band, *others)
    return update[None], new[None, None]


def solution(mesh):
    fine = Mesh(mesh.devices.reshape(4, 2, 4, 4, 2), ("rep", "zh", "x", "y", "core"))
    every = ("rep", "zh", "x", "y", "core")
    return jax.shard_map(
        on_device,
        mesh=fine,
        in_specs=(
            P(None, every, None),
            P(None, every, None),
            P("rep", None, every[1:], None),
        ),
        out_specs=(P(None, every[1:], None), P("rep", None, every[1:], None)),
        check_vma=False,
    )
```

```python
import functools

import jax
import jax.numpy as jnp
import numpy as np
from jax import lax
from jax.experimental import pallas as pl
from jax.experimental.pallas import tpu as pltpu
from jax.sharding import Mesh
from jax.sharding import PartitionSpec as P

SPAN = 64
BAND = 8
LANES = 128
GROUP = 1024
DECAY = 0.9
CHUNK_TILES = (4, 4, 3)
PARAMS = pltpu.CompilerParams(vmem_limit_bytes=56 << 20)
ANY = pl.BlockSpec(memory_space=pl.ANY)
QUICK = pl.CostEstimate(flops=1, bytes_accessed=1, transcendentals=0)
SMEM = pl.BlockSpec(memory_space=pltpu.SMEM)
VMEM = pl.BlockSpec(memory_space=pltpu.VMEM)


def band_table():
    freqs = np.arange(BAND, dtype=np.float64)[:, None]
    points = np.arange(SPAN, dtype=np.float64)[None, :]
    scales = np.where(freqs == 0.0, np.sqrt(1.0 / SPAN), np.sqrt(2.0 / SPAN))
    return (scales * np.cos(np.pi * (2.0 * points + 1.0) * freqs / (2.0 * SPAN))).astype(np.float32)


def shift(n, by):
    return [(i, (i + by) % n) for i in range(n)]


def halved(value):
    high = value.astype(jnp.bfloat16)
    return high, (value - high.astype(jnp.float32)).astype(jnp.bfloat16)


def dot(a, b):
    (ah, al), (bh, bl) = halved(a), halved(b)
    return jnp.dot(
        jnp.concatenate([ah, ah, al], axis=1),
        jnp.concatenate([bh, bl, bh], axis=0),
        preferred_element_type=jnp.float32,
    )


def groups_of(width):
    return [(start, min(GROUP, width - start)) for start in range(0, width, GROUP)]


def starts_of(width, block):
    return [min(j * block, width - block) for j in range(8)]


def finish_kernel(widths, basis_ref, back_ref, wide_ref, tall_ref, mom_ref, *refs):
    n = len(widths)
    pieces, (new_ref, band_ref, rows_ref) = refs[:n], refs[n:]
    width = mom_ref.shape[1]
    for j, start in enumerate(starts_of(width, sum(widths))):
        for k, w in enumerate(widths):
            at = pl.ds(start + sum(widths[:k]), w)
            new_ref[:, at] = DECAY * mom_ref[:, at] + pieces[k][j]
    rows_ref[...] = jnp.zeros_like(rows_ref)
    for i, (start, w) in enumerate(groups_of(width)):
        rows_ref[i * BAND : (i + 1) * BAND, :w] = dot(basis_ref[...], new_ref[:, start : start + w])
    band = dot(rows_ref[...], wide_ref[...])
    band_ref[...] = band
    rows_ref[...] = dot(band, tall_ref[...])
    for i, (start, w) in enumerate(groups_of(width)):
        new_ref[:, start : start + w] -= dot(back_ref[...], rows_ref[i * BAND : (i + 1) * BAND, :w])


def update_kernel(back_ref, tall_ref, b0, b1, b2, b3, out_ref):
    total = ((b0[...] + b1[...]) + (b2[...] + b3[...])) * 0.25
    rows = dot(total, tall_ref[...])
    for i, (start, w) in enumerate(groups_of(out_ref.shape[1])):
        out_ref[:, start : start + w] = dot(back_ref[...], rows[i * BAND : (i + 1) * BAND, :w])


def call(kernel, out, *args, spec=None):
    shapes = [jax.ShapeDtypeStruct(s, t) for s, t in out]
    return pl.pallas_call(
        kernel,
        out_shape=shapes,
        in_specs=spec or [VMEM] * len(args),
        out_specs=[VMEM] * len(out),
        compiler_params=PARAMS,
        cost_estimate=QUICK,
    )(*args)


def strips_kernel(half, at_ref, acts_ref, *outs):
    for e, out in enumerate(outs):
        for i in range(2):
            at = pl.ds(pl.multiple_of(at_ref[2 * e + i], LANES), half)
            out[i * half : (i + 1) * half] = acts_ref[:, at].T


def blocks_kernel(starts, leads, units_ref, *outs):
    for lead, out in zip(leads, outs):
        for j, start in enumerate(starts):
            out[j] = units_ref[:, start + lead : start + lead + out.shape[2]]


def blocks(units, starts, leads, widths):
    outs = [((8, units.shape[0], w), units.dtype) for w in widths]
    return call(functools.partial(blocks_kernel, starts, leads), outs, units)


def product(left, rights):
    total = None
    for i, some in enumerate(((0,), (1,), (2,), (3, 4))):
        count = 8 // len(some)
        for m, n in enumerate(some):
            part = jnp.concatenate([left[count * m + j, i] for j in range(count)], axis=1)
            term = jnp.dot(part, rights[n][...], preferred_element_type=jnp.float32)
            total = term if total is None else total + term
    return total


def keep_kernel(left_ref, *refs):
    refs[5][...] = product(left_ref, refs[:5])


def send_kernel(left_ref, *refs):
    rights, out, top_ref = refs[:5], refs[5], refs[6]
    i, rows = pl.program_id(0), left_ref.shape[2]
    value = product(left_ref, rights)
    top = jnp.max(jnp.max(jnp.abs(value), axis=0, keepdims=True), axis=1, keepdims=True)

    @pl.when(i == 0)
    def _():
        top_ref[...] = jnp.zeros_like(top_ref)

    top_ref[...] = jnp.maximum(top_ref[...], top)
    out[pl.ds(pl.multiple_of(i * rows, rows), rows)] = value

    @pl.when(i == pl.num_programs(0) - 1)
    def _():
        half, w = out.shape[0] - 16, out.shape[1]
        power = jnp.floor(15.0 - jnp.log2(jnp.maximum(top_ref[:1, :1], 2.0**-100)))
        out[:half] = out[:half] * jnp.exp2(power)
        out[half:] = jnp.broadcast_to(power, (16, w))


def tile(kernel, lefts, rights, extra):
    n, dx, half, tok = lefts.shape
    w = rights[0].shape[1]
    rows = 256
    if extra:
        out_spec = pl.BlockSpec((half + extra, w), lambda i: (0, 0))
        scratch = [pltpu.VMEM((8, LANES), jnp.float32)]
    else:
        out_spec = pl.BlockSpec((rows, w), lambda i: (i, 0))
        scratch = []
    in_specs = [pl.BlockSpec((n, dx, rows, tok), lambda i: (0, 0, i, 0))]
    depth = rights[0].shape[0]
    for n, b in enumerate(rights):
        size = depth if n < 3 else depth // 2
        place = 0 if n < 3 else b.shape[0] // size - 1
        in_specs.append(pl.BlockSpec((size, w), lambda i, place=place: (place, 0)))
    return pl.pallas_call(
        kernel,
        grid=(half // rows,),
        out_shape=jax.ShapeDtypeStruct((half + extra, w), jnp.float32),
        in_specs=in_specs,
        out_specs=out_spec,
        scratch_shapes=scratch,
        compiler_params=PARAMS,
        cost_estimate=QUICK,
    )(lefts, *rights)


def join_kernel(*refs):
    out, lead = refs[-1], 0
    for keep_ref, got_ref in zip(refs[:-1:2], refs[1:-1:2]):
        half, w = keep_ref.shape
        scale = jnp.exp2(-got_ref[half : half + 1, :1])
        out[:, lead : lead + w] = keep_ref[...] + got_ref[:half] * scale
        lead += w


def on_device(activations, unit_grads, momentum):
    acts, units, mom = activations[0], unit_grads[0], momentum[0, 0]
    tok, features = acts.shape
    width = units.shape[1]
    zh, x = lax.axis_index("zh"), lax.axis_index("x")
    plane_rows = features // 2
    half = plane_rows // 4
    own_rows = half // 8
    block = -(-width // (8 * LANES)) * LANES
    widths = [LANES * t for t in CHUNK_TILES]
    f32, b16 = jnp.float32, acts.dtype

    def along(axis, by, value):
        return lax.ppermute(value, axis, shift(2 if axis in ("core", "zh") else 4, by))

    def sync(*values):
        return lax.optimization_barrier(values)

    def swap(value):
        return lax.all_to_all(value, ("y", "core"), 0, 0, tiled=True)

    def column_block(cut):
        return swap(cut).reshape(8 * tok, cut.shape[2])

    def ring(v):
        return along("x", 1, v), along("x", 3, v)

    def halves(r, l):
        depth = 4 * tok
        return r[:depth], l[depth : 2 * depth]

    def payload(sent, five):
        return tile(send_kernel, sent, five, 16).astype(jnp.float16)

    def joined(keep, got):
        other = got[:half].astype(f32) * jnp.exp2(-got[half : half + 1].astype(f32))
        return (keep + other).reshape(8, own_rows, keep.shape[1])

    strips_at = jnp.stack(
        [plane_rows * p + half * ((x + e) % 4) for e in range(4) for p in (zh, 1 - zh)]
    ).astype(jnp.int32)

    starts = starts_of(width, block)
    leads = [sum(widths[:k]) for k in range(len(widths))]

    (cut0,) = blocks(units, starts, leads[:1], widths[:1])
    v0 = column_block(cut0)
    s0, s1, s2, s3 = call(
        functools.partial(strips_kernel, half), [((2 * half, tok), b16)] * 4, strips_at, acts, spec=[SMEM, VMEM]
    )
    local = [s0, along("x", 1, s1), along("x", 3, s3), along("x", 2, s2)]
    kept = jnp.stack([a[:half] for a in local])
    sent = jnp.stack([a[half:] for a in local])

    v0, sent, units = sync(v0, sent, units)
    r0, l0 = ring(v0)
    cut1, cut2 = blocks(units, starts, leads[1:], widths[1:])
    v1 = column_block(cut1)

    v1, r0, l0, sent, kept, cut2 = sync(v1, r0, l0, sent, kept, cut2)
    far_r, far_l = halves(r0, l0)
    right, left = jnp.concatenate([v1, far_r]), jnp.concatenate([v1, far_l])
    right, left, sent, kept, cut2 = sync(right, left, sent, kept, cut2)
    r1, l1 = along("x", 1, right), along("x", 3, left)
    v2 = column_block(cut2)
    sent = lax.all_gather(sent, ("y", "core"))

    r1, l1, v2, sent, kept = sync(r1, l1, v2, sent, kept)
    half1 = halves(r1, l1)
    half1, r1, l1, v2, sent, kept = sync(half1, r1, l1, v2, sent, kept)
    far1 = along("x", 1, half1[0]), along("x", 3, half1[1])
    r2, l2 = ring(v2)
    send0 = payload(sent, [v0, r0, l0, r1, l1])
    kept = lax.all_gather(kept, ("y", "core"))

    send0, sent = sync(send0, sent)
    got0 = along("zh", 1, send0)
    send1 = payload(sent, [v1, r1, l1, *far1])

    r2, l2, got0, send1, kept = sync(r2, l2, got0, send1, kept)
    half2 = halves(r2, l2)
    half2, got0, send1, kept = sync(half2, got0, send1, kept)
    far2 = along("x", 1, half2[0]), along("x", 3, half2[1])
    got1 = along("zh", 1, send1)
    send2 = payload(sent, [v2, r2, l2, *far2])
    total0 = joined(tile(keep_kernel, kept, [v0, r0, l0, r1, l1], 0), got0)

    got1, send2, total0, kept = sync(got1, send2, total0, kept)
    got2 = along("zh", 1, send2)
    done0 = swap(total0)
    keep1 = tile(keep_kernel, kept, [v1, r1, l1, *far1], 0)
    keep2 = tile(keep_kernel, kept, [v2, r2, l2, *far2], 0)
    other1 = got1.astype(f32)

    got2, done0, keep1, keep2, other1 = sync(got2, done0, keep1, keep2, other1)
    late = block - widths[0]
    (total,) = call(join_kernel, [((half, late), f32)], keep1, other1, keep2, got2.astype(f32))
    done = [done0, swap(total.reshape(8, own_rows, late))]

    basis = band_table()
    wide = np.kron(np.eye(GROUP // SPAN, dtype=np.float32), basis.T)
    rows = len(groups_of(width)) * BAND
    with jax.named_scope("finish"):
        new, band = pl.pallas_call(
            functools.partial(finish_kernel, [d.shape[2] for d in done]),
            out_shape=(
                jax.ShapeDtypeStruct(mom.shape, f32),
                jax.ShapeDtypeStruct((rows, LANES), f32),
            ),
            in_specs=[VMEM] * (5 + len(done)),
            out_specs=(VMEM, VMEM),
            scratch_shapes=[pltpu.VMEM((rows, GROUP), f32)],
            compiler_params=PARAMS,
        )(basis, basis.T, wide, wide.T, mom, *done)
    with jax.named_scope("band"):
        others = [along("rep", s, band) for s in (1, 2, 3)]
    with jax.named_scope("update"):
        (update,) = call(update_kernel, [(mom.shape, f32)], jnp.asarray(basis.T), jnp.asarray(wide.T), band, *others)
    return update[None], new[None, None]


def solution(mesh):
    fine = Mesh(mesh.devices.reshape(4, 2, 4, 4, 2), ("rep", "zh", "x", "y", "core"))
    every = ("rep", "zh", "x", "y", "core")
    return jax.shard_map(
        on_device,
        mesh=fine,
        in_specs=(
            P(None, every, None),
            P(None, every, None),
            P("rep", None, every[1:], None),
        ),
        out_specs=(P(None, every[1:], None), P("rep", None, every[1:], None)),
        check_vma=False,
    )
```

```python
import functools

import jax
import jax.numpy as jnp
import numpy as np
from jax import lax
from jax.experimental import pallas as pl
from jax.experimental.pallas import tpu as pltpu
from jax.sharding import Mesh
from jax.sharding import PartitionSpec as P

SPAN = 64
BAND = 8
LANES = 128
GROUP = 1024
DECAY = 0.9
CHUNK_TILES = (4, 4, 3)
PARAMS = pltpu.CompilerParams(vmem_limit_bytes=56 << 20)
ANY = pl.BlockSpec(memory_space=pl.ANY)
QUICK = pl.CostEstimate(flops=1, bytes_accessed=1, transcendentals=0)
SMEM = pl.BlockSpec(memory_space=pltpu.SMEM)
VMEM = pl.BlockSpec(memory_space=pltpu.VMEM)


def band_table():
    freqs = np.arange(BAND, dtype=np.float64)[:, None]
    points = np.arange(SPAN, dtype=np.float64)[None, :]
    scales = np.where(freqs == 0.0, np.sqrt(1.0 / SPAN), np.sqrt(2.0 / SPAN))
    return (scales * np.cos(np.pi * (2.0 * points + 1.0) * freqs / (2.0 * SPAN))).astype(np.float32)


def shift(n, by):
    return [(i, (i + by) % n) for i in range(n)]


def halved(value):
    high = value.astype(jnp.bfloat16)
    return high, (value - high.astype(jnp.float32)).astype(jnp.bfloat16)


def dot(a, b):
    (ah, al), (bh, bl) = halved(a), halved(b)
    return jnp.dot(
        jnp.concatenate([ah, ah, al], axis=1),
        jnp.concatenate([bh, bl, bh], axis=0),
        preferred_element_type=jnp.float32,
    )


def groups_of(width):
    return [(start, min(GROUP, width - start)) for start in range(0, width, GROUP)]


def starts_of(width, block):
    return [min(j * block, width - block) for j in range(8)]


def finish_kernel(widths, basis_ref, back_ref, wide_ref, tall_ref, mom_ref, *refs):
    n = len(widths)
    pieces, (new_ref, band_ref, rows_ref) = refs[:n], refs[n:]
    width = mom_ref.shape[1]
    for j, start in enumerate(starts_of(width, sum(widths))):
        for k, w in enumerate(widths):
            at = pl.ds(start + sum(widths[:k]), w)
            new_ref[:, at] = DECAY * mom_ref[:, at] + pieces[k][j]
    rows_ref[...] = jnp.zeros_like(rows_ref)
    for i, (start, w) in enumerate(groups_of(width)):
        rows_ref[i * BAND : (i + 1) * BAND, :w] = dot(basis_ref[...], new_ref[:, start : start + w])
    band = dot(rows_ref[...], wide_ref[...])
    band_ref[...] = band
    rows_ref[...] = dot(band, tall_ref[...])
    for i, (start, w) in enumerate(groups_of(width)):
        new_ref[:, start : start + w] -= dot(back_ref[...], rows_ref[i * BAND : (i + 1) * BAND, :w])


def update_kernel(back_ref, tall_ref, b0, b1, b2, b3, out_ref):
    total = ((b0[...] + b1[...]) + (b2[...] + b3[...])) * 0.25
    rows = dot(total, tall_ref[...])
    for i, (start, w) in enumerate(groups_of(out_ref.shape[1])):
        out_ref[:, start : start + w] = dot(back_ref[...], rows[i * BAND : (i + 1) * BAND, :w])


def call(kernel, out, *args, spec=None):
    shapes = [jax.ShapeDtypeStruct(s, t) for s, t in out]
    return pl.pallas_call(
        kernel,
        out_shape=shapes,
        in_specs=spec or [VMEM] * len(args),
        out_specs=[VMEM] * len(out),
        compiler_params=PARAMS,
        cost_estimate=QUICK,
    )(*args)


def strips_kernel(half, at_ref, acts_ref, *outs):
    for e, out in enumerate(outs):
        for i in range(2):
            at = pl.ds(pl.multiple_of(at_ref[2 * e + i], LANES), half)
            out[i * half : (i + 1) * half] = acts_ref[:, at].T


def blocks_kernel(starts, leads, units_ref, *outs):
    for lead, out in zip(leads, outs):
        for j, start in enumerate(starts):
            out[j] = units_ref[:, start + lead : start + lead + out.shape[2]]


def blocks(units, starts, leads, widths):
    outs = [((8, units.shape[0], w), units.dtype) for w in widths]
    return call(functools.partial(blocks_kernel, starts, leads), outs, units)


def product(left, rights):
    total = None
    for i, some in enumerate(((0,), (1,), (2,), (3, 4))):
        count = 8 // len(some)
        for m, n in enumerate(some):
            part = jnp.concatenate([left[count * m + j, i] for j in range(count)], axis=1)
            term = jnp.dot(part, rights[n][...], preferred_element_type=jnp.float32)
            total = term if total is None else total + term
    return total


def keep_kernel(left_ref, *refs):
    refs[5][...] = product(left_ref, refs[:5])


def send_kernel(left_ref, *refs):
    rights, out, top_ref = refs[:5], refs[5], refs[6]
    i, rows = pl.program_id(0), left_ref.shape[2]
    value = product(left_ref, rights)
    top = jnp.max(jnp.max(jnp.abs(value), axis=0, keepdims=True), axis=1, keepdims=True)

    @pl.when(i == 0)
    def _():
        top_ref[...] = jnp.zeros_like(top_ref)

    top_ref[...] = jnp.maximum(top_ref[...], top)
    out[pl.ds(pl.multiple_of(i * rows, rows), rows)] = value

    @pl.when(i == pl.num_programs(0) - 1)
    def _():
        half, w = out.shape[0] - 16, out.shape[1]
        power = jnp.floor(15.0 - jnp.log2(jnp.maximum(top_ref[:1, :1], 2.0**-100)))
        out[:half] = out[:half] * jnp.exp2(power)
        out[half:] = jnp.broadcast_to(power, (16, w))


def tile(kernel, lefts, rights, extra):
    n, dx, half, tok = lefts.shape
    w = rights[0].shape[1]
    rows = 256
    if extra:
        out_spec = pl.BlockSpec((half + extra, w), lambda i: (0, 0))
        scratch = [pltpu.VMEM((8, LANES), jnp.float32)]
    else:
        out_spec = pl.BlockSpec((rows, w), lambda i: (i, 0))
        scratch = []
    in_specs = [pl.BlockSpec((n, dx, rows, tok), lambda i: (0, 0, i, 0))]
    depth = rights[0].shape[0]
    for n, b in enumerate(rights):
        size = depth if n < 3 else depth // 2
        place = 0 if n < 3 else b.shape[0] // size - 1
        in_specs.append(pl.BlockSpec((size, w), lambda i, place=place: (place, 0)))
    return pl.pallas_call(
        kernel,
        grid=(half // rows,),
        out_shape=jax.ShapeDtypeStruct((half + extra, w), jnp.float32),
        in_specs=in_specs,
        out_specs=out_spec,
        scratch_shapes=scratch,
        compiler_params=PARAMS,
        cost_estimate=QUICK,
    )(lefts, *rights)


def join_kernel(*refs):
    out, lead = refs[-1], 0
    for keep_ref, got_ref in zip(refs[:-1:2], refs[1:-1:2]):
        half, w = keep_ref.shape
        scale = jnp.exp2(-got_ref[half : half + 1, :1])
        out[:, lead : lead + w] = keep_ref[...] + got_ref[:half] * scale
        lead += w


def on_device(activations, unit_grads, momentum):
    acts, units, mom = activations[0], unit_grads[0], momentum[0, 0]
    tok, features = acts.shape
    width = units.shape[1]
    zh, x = lax.axis_index("zh"), lax.axis_index("x")
    plane_rows = features // 2
    half = plane_rows // 4
    own_rows = half // 8
    block = -(-width // (8 * LANES)) * LANES
    widths = [LANES * t for t in CHUNK_TILES]
    f32, b16 = jnp.float32, acts.dtype

    def along(axis, by, value):
        return lax.ppermute(value, axis, shift(2 if axis in ("core", "zh") else 4, by))

    def sync(*values):
        return lax.optimization_barrier(values)

    def swap(value):
        return lax.all_to_all(value, ("y", "core"), 0, 0, tiled=True)

    def column_block(cut):
        return swap(cut).reshape(8 * tok, cut.shape[2])

    def ring(v):
        return along("x", 1, v), along("x", 3, v)

    def halves(r, l):
        depth = 4 * tok
        return r[:depth], l[depth : 2 * depth]

    def payload(sent, five):
        return tile(send_kernel, sent, five, 16).astype(jnp.float16)

    def joined(keep, got):
        other = got[:half].astype(f32) * jnp.exp2(-got[half : half + 1].astype(f32))
        return (keep + other).reshape(8, own_rows, keep.shape[1])

    strips_at = jnp.stack(
        [plane_rows * p + half * ((x + e) % 4) for e in range(4) for p in (zh, 1 - zh)]
    ).astype(jnp.int32)

    starts = starts_of(width, block)
    leads = [sum(widths[:k]) for k in range(len(widths))]

    (cut0,) = blocks(units, starts, leads[:1], widths[:1])
    v0 = column_block(cut0)
    s0, s1, s2, s3 = call(
        functools.partial(strips_kernel, half), [((2 * half, tok), b16)] * 4, strips_at, acts, spec=[SMEM, VMEM]
    )
    local = [s0, along("x", 1, s1), along("x", 3, s3), along("x", 2, s2)]
    kept = jnp.stack([a[:half] for a in local])
    sent = jnp.stack([a[half:] for a in local])

    v0, sent, units = sync(v0, sent, units)
    r0, l0 = ring(v0)
    cut1, cut2 = blocks(units, starts, leads[1:], widths[1:])
    v1 = column_block(cut1)

    v1, r0, l0, sent, kept, cut2 = sync(v1, r0, l0, sent, kept, cut2)
    far_r, far_l = halves(r0, l0)
    right, left = jnp.concatenate([v1, far_r]), jnp.concatenate([v1, far_l])
    right, left, sent, kept, cut2 = sync(right, left, sent, kept, cut2)
    r1, l1 = along("x", 1, right), along("x", 3, left)
    v2 = column_block(cut2)
    sent = lax.all_gather(sent, ("y", "core"))

    r1, l1, v2, sent, kept = sync(r1, l1, v2, sent, kept)
    half1 = halves(r1, l1)
    half1, r1, l1, v2, sent, kept = sync(half1, r1, l1, v2, sent, kept)
    far1 = along("x", 1, half1[0]), along("x", 3, half1[1])
    r2, l2 = ring(v2)
    send0 = payload(sent, [v0, r0, l0, r1, l1])
    kept = lax.all_gather(kept, ("y", "core"))

    send0, sent = sync(send0, sent)
    got0 = along("zh", 1, send0)
    send1 = payload(sent, [v1, r1, l1, *far1])

    r2, l2, send1, kept = sync(r2, l2, send1, kept)
    half2 = halves(r2, l2)
    half2, send1, kept = sync(half2, send1, kept)
    far2 = along("x", 1, half2[0]), along("x", 3, half2[1])
    got1 = along("zh", 1, send1)
    send2 = payload(sent, [v2, r2, l2, *far2])
    kept, got0 = sync(kept, got0)
    total0 = joined(tile(keep_kernel, kept, [v0, r0, l0, r1, l1], 0), got0)

    got1, send2, total0, kept = sync(got1, send2, total0, kept)
    got2 = along("zh", 1, send2)
    done0 = swap(total0)
    keep1 = tile(keep_kernel, kept, [v1, r1, l1, *far1], 0)
    keep2 = tile(keep_kernel, kept, [v2, r2, l2, *far2], 0)
    other1 = got1.astype(f32)

    got2, done0, keep1, keep2, other1 = sync(got2, done0, keep1, keep2, other1)
    late = block - widths[0]
    (total,) = call(join_kernel, [((half, late), f32)], keep1, other1, keep2, got2.astype(f32))
    done = [done0, swap(total.reshape(8, own_rows, late))]

    basis = band_table()
    wide = np.kron(np.eye(GROUP // SPAN, dtype=np.float32), basis.T)
    rows = len(groups_of(width)) * BAND
    with jax.named_scope("finish"):
        new, band = pl.pallas_call(
            functools.partial(finish_kernel, [d.shape[2] for d in done]),
            out_shape=(
                jax.ShapeDtypeStruct(mom.shape, f32),
                jax.ShapeDtypeStruct((rows, LANES), f32),
            ),
            in_specs=[VMEM] * (5 + len(done)),
            out_specs=(VMEM, VMEM),
            scratch_shapes=[pltpu.VMEM((rows, GROUP), f32)],
            compiler_params=PARAMS,
        )(basis, basis.T, wide, wide.T, mom, *done)
    with jax.named_scope("band"):
        others = [along("rep", s, band) for s in (1, 2, 3)]
    with jax.named_scope("update"):
        (update,) = call(update_kernel, [(mom.shape, f32)], jnp.asarray(basis.T), jnp.asarray(wide.T), band, *others)
    return update[None], new[None, None]


def solution(mesh):
    fine = Mesh(mesh.devices.reshape(4, 2, 4, 4, 2), ("rep", "zh", "x", "y", "core"))
    every = ("rep", "zh", "x", "y", "core")
    return jax.shard_map(
        on_device,
        mesh=fine,
        in_specs=(
            P(None, every, None),
            P(None, every, None),
            P("rep", None, every[1:], None),
        ),
        out_specs=(P(None, every[1:], None), P("rep", None, every[1:], None)),
        check_vma=False,
    )
```

```python
import functools

import jax
import jax.numpy as jnp
import numpy as np
from jax import lax
from jax.experimental import pallas as pl
from jax.experimental.pallas import tpu as pltpu
from jax.sharding import Mesh
from jax.sharding import PartitionSpec as P

SPAN = 64
BAND = 8
LANES = 128
GROUP = 1024
DECAY = 0.9
CHUNK_TILES = (4, 4, 3)
PARAMS = pltpu.CompilerParams(vmem_limit_bytes=56 << 20)
ANY = pl.BlockSpec(memory_space=pl.ANY)
QUICK = pl.CostEstimate(flops=1, bytes_accessed=1, transcendentals=0)
SMEM = pl.BlockSpec(memory_space=pltpu.SMEM)
VMEM = pl.BlockSpec(memory_space=pltpu.VMEM)


def band_table():
    freqs = np.arange(BAND, dtype=np.float64)[:, None]
    points = np.arange(SPAN, dtype=np.float64)[None, :]
    scales = np.where(freqs == 0.0, np.sqrt(1.0 / SPAN), np.sqrt(2.0 / SPAN))
    return (scales * np.cos(np.pi * (2.0 * points + 1.0) * freqs / (2.0 * SPAN))).astype(np.float32)


def shift(n, by):
    return [(i, (i + by) % n) for i in range(n)]


def halved(value):
    high = value.astype(jnp.bfloat16)
    return high, (value - high.astype(jnp.float32)).astype(jnp.bfloat16)


def dot(a, b):
    (ah, al), (bh, bl) = halved(a), halved(b)
    return jnp.dot(
        jnp.concatenate([ah, ah, al], axis=1),
        jnp.concatenate([bh, bl, bh], axis=0),
        preferred_element_type=jnp.float32,
    )


def groups_of(width):
    return [(start, min(GROUP, width - start)) for start in range(0, width, GROUP)]


def starts_of(width, block):
    return [min(j * block, width - block) for j in range(8)]


def finish_kernel(widths, basis_ref, back_ref, wide_ref, tall_ref, mom_ref, *refs):
    n = len(widths)
    pieces, (new_ref, band_ref, rows_ref) = refs[:n], refs[n:]
    width = mom_ref.shape[1]
    for j, start in enumerate(starts_of(width, sum(widths))):
        for k, w in enumerate(widths):
            at = pl.ds(start + sum(widths[:k]), w)
            new_ref[:, at] = DECAY * mom_ref[:, at] + pieces[k][j]
    rows_ref[...] = jnp.zeros_like(rows_ref)
    for i, (start, w) in enumerate(groups_of(width)):
        rows_ref[i * BAND : (i + 1) * BAND, :w] = dot(basis_ref[...], new_ref[:, start : start + w])
    band = dot(rows_ref[...], wide_ref[...])
    band_ref[...] = band
    rows_ref[...] = dot(band, tall_ref[...])
    for i, (start, w) in enumerate(groups_of(width)):
        new_ref[:, start : start + w] -= dot(back_ref[...], rows_ref[i * BAND : (i + 1) * BAND, :w])


def update_kernel(back_ref, tall_ref, b0, b1, b2, b3, out_ref):
    total = ((b0[...] + b1[...]) + (b2[...] + b3[...])) * 0.25
    rows = dot(total, tall_ref[...])
    for i, (start, w) in enumerate(groups_of(out_ref.shape[1])):
        out_ref[:, start : start + w] = dot(back_ref[...], rows[i * BAND : (i + 1) * BAND, :w])


def call(kernel, out, *args, spec=None):
    shapes = [jax.ShapeDtypeStruct(s, t) for s, t in out]
    return pl.pallas_call(
        kernel,
        out_shape=shapes,
        in_specs=spec or [VMEM] * len(args),
        out_specs=[VMEM] * len(out),
        compiler_params=PARAMS,
        cost_estimate=QUICK,
    )(*args)


def strips_kernel(half, at_ref, acts_ref, *outs):
    for e, out in enumerate(outs):
        for i in range(2):
            at = pl.ds(pl.multiple_of(at_ref[2 * e + i], LANES), half)
            out[i * half : (i + 1) * half] = acts_ref[:, at].T


def blocks_kernel(starts, leads, units_ref, *outs):
    for lead, out in zip(leads, outs):
        for j, start in enumerate(starts):
            out[j] = units_ref[:, start + lead : start + lead + out.shape[2]]


def blocks(units, starts, leads, widths):
    outs = [((8, units.shape[0], w), units.dtype) for w in widths]
    return call(functools.partial(blocks_kernel, starts, leads), outs, units)


def product(left, rights):
    total = None
    for i, some in enumerate(((0,), (1,), (2,), (3, 4))):
        count = 8 // len(some)
        for m, n in enumerate(some):
            part = jnp.concatenate([left[count * m + j, i] for j in range(count)], axis=1)
            term = jnp.dot(part, rights[n][...], preferred_element_type=jnp.float32)
            total = term if total is None else total + term
    return total


def keep_kernel(left_ref, *refs):
    refs[5][...] = product(left_ref, refs[:5])


def send_kernel(left_ref, *refs):
    rights, out, top_ref = refs[:5], refs[5], refs[6]
    i, rows = pl.program_id(0), left_ref.shape[2]
    value = product(left_ref, rights)
    top = jnp.max(jnp.max(jnp.abs(value), axis=0, keepdims=True), axis=1, keepdims=True)

    @pl.when(i == 0)
    def _():
        top_ref[...] = jnp.zeros_like(top_ref)

    top_ref[...] = jnp.maximum(top_ref[...], top)
    out[pl.ds(pl.multiple_of(i * rows, rows), rows)] = value

    @pl.when(i == pl.num_programs(0) - 1)
    def _():
        half, w = out.shape[0] - 16, out.shape[1]
        power = jnp.floor(15.0 - jnp.log2(jnp.maximum(top_ref[:1, :1], 2.0**-100)))
        out[:half] = out[:half] * jnp.exp2(power)
        out[half:] = jnp.broadcast_to(power, (16, w))


def tile(kernel, lefts, rights, extra):
    n, dx, half, tok = lefts.shape
    w = rights[0].shape[1]
    rows = 256
    if extra:
        out_spec = pl.BlockSpec((half + extra, w), lambda i: (0, 0))
        scratch = [pltpu.VMEM((8, LANES), jnp.float32)]
    else:
        out_spec = pl.BlockSpec((rows, w), lambda i: (i, 0))
        scratch = []
    in_specs = [pl.BlockSpec((n, dx, rows, tok), lambda i: (0, 0, i, 0))]
    depth = rights[0].shape[0]
    for n, b in enumerate(rights):
        size = depth if n < 3 else depth // 2
        place = 0 if n < 3 else b.shape[0] // size - 1
        in_specs.append(pl.BlockSpec((size, w), lambda i, place=place: (place, 0)))
    return pl.pallas_call(
        kernel,
        grid=(half // rows,),
        out_shape=jax.ShapeDtypeStruct((half + extra, w), jnp.float32),
        in_specs=in_specs,
        out_specs=out_spec,
        scratch_shapes=scratch,
        compiler_params=PARAMS,
        cost_estimate=QUICK,
    )(lefts, *rights)


def join_kernel(*refs):
    out, lead = refs[-1], 0
    for keep_ref, got_ref in zip(refs[:-1:2], refs[1:-1:2]):
        half, w = keep_ref.shape
        scale = jnp.exp2(-got_ref[half : half + 1, :1])
        out[:, lead : lead + w] = keep_ref[...] + got_ref[:half] * scale
        lead += w


def on_device(activations, unit_grads, momentum):
    acts, units, mom = activations[0], unit_grads[0], momentum[0, 0]
    tok, features = acts.shape
    width = units.shape[1]
    zh, x = lax.axis_index("zh"), lax.axis_index("x")
    plane_rows = features // 2
    half = plane_rows // 4
    own_rows = half // 8
    block = -(-width // (8 * LANES)) * LANES
    widths = [LANES * t for t in CHUNK_TILES]
    f32, b16 = jnp.float32, acts.dtype

    def along(axis, by, value):
        return lax.ppermute(value, axis, shift(2 if axis in ("core", "zh") else 4, by))

    def sync(*values):
        return lax.optimization_barrier(values)

    def swap(value):
        return lax.all_to_all(value, ("y", "core"), 0, 0, tiled=True)

    def column_block(cut):
        return swap(cut).reshape(8 * tok, cut.shape[2])

    def ring(v):
        return along("x", 1, v), along("x", 3, v)

    def halves(r, l):
        depth = 4 * tok
        return r[:depth], l[depth : 2 * depth]

    def payload(sent, five):
        return tile(send_kernel, sent, five, 16).astype(jnp.float16)

    def joined(keep, got):
        other = got[:half].astype(f32) * jnp.exp2(-got[half : half + 1].astype(f32))
        return (keep + other).reshape(8, own_rows, keep.shape[1])

    strips_at = jnp.stack(
        [plane_rows * p + half * ((x + e) % 4) for e in range(4) for p in (zh, 1 - zh)]
    ).astype(jnp.int32)

    starts = starts_of(width, block)
    leads = [sum(widths[:k]) for k in range(len(widths))]

    (cut0,) = blocks(units, starts, leads[:1], widths[:1])
    v0 = column_block(cut0)
    s0, s1, s2, s3 = call(
        functools.partial(strips_kernel, half), [((2 * half, tok), b16)] * 4, strips_at, acts, spec=[SMEM, VMEM]
    )
    local = [s0, along("x", 1, s1), along("x", 3, s3), along("x", 2, s2)]
    kept = jnp.stack([a[:half] for a in local])
    sent = jnp.stack([a[half:] for a in local])

    v0, sent, units = sync(v0, sent, units)
    r0, l0 = ring(v0)
    cut1, cut2 = blocks(units, starts, leads[1:], widths[1:])
    v1 = column_block(cut1)

    v1, r0, l0, sent, kept, cut2 = sync(v1, r0, l0, sent, kept, cut2)
    far_r, far_l = halves(r0, l0)
    right, left = jnp.concatenate([v1, far_r]), jnp.concatenate([v1, far_l])
    right, left, sent, kept, cut2 = sync(right, left, sent, kept, cut2)
    r1, l1 = along("x", 1, right), along("x", 3, left)
    v2 = column_block(cut2)
    sent = lax.all_gather(sent, ("y", "core"))

    r1, l1, v2, sent, kept = sync(r1, l1, v2, sent, kept)
    half1 = halves(r1, l1)
    half1, r1, l1, v2, sent, kept = sync(half1, r1, l1, v2, sent, kept)
    far1 = along("x", 1, half1[0]), along("x", 3, half1[1])
    send0 = payload(sent, [v0, r0, l0, r1, l1])
    kept = lax.all_gather(kept, ("y", "core"))

    far1, send0, v2, sent = sync(far1, send0, v2, sent)
    r2, l2 = ring(v2)
    got0 = along("zh", 1, send0)
    send1 = payload(sent, [v1, r1, l1, *far1])

    r2, l2, send1, kept = sync(r2, l2, send1, kept)
    half2 = halves(r2, l2)
    half2, send1, kept = sync(half2, send1, kept)
    far2 = along("x", 1, half2[0]), along("x", 3, half2[1])
    got1 = along("zh", 1, send1)
    send2 = payload(sent, [v2, r2, l2, *far2])
    kept, got0 = sync(kept, got0)
    total0 = joined(tile(keep_kernel, kept, [v0, r0, l0, r1, l1], 0), got0)

    got1, send2, total0, kept = sync(got1, send2, total0, kept)
    got2 = along("zh", 1, send2)
    done0 = swap(total0)
    keep1 = tile(keep_kernel, kept, [v1, r1, l1, *far1], 0)
    keep2 = tile(keep_kernel, kept, [v2, r2, l2, *far2], 0)
    other1 = got1.astype(f32)

    got2, done0, keep1, keep2, other1 = sync(got2, done0, keep1, keep2, other1)
    late = block - widths[0]
    (total,) = call(join_kernel, [((half, late), f32)], keep1, other1, keep2, got2.astype(f32))
    done = [done0, swap(total.reshape(8, own_rows, late))]

    basis = band_table()
    wide = np.kron(np.eye(GROUP // SPAN, dtype=np.float32), basis.T)
    rows = len(groups_of(width)) * BAND
    with jax.named_scope("finish"):
        new, band = pl.pallas_call(
            functools.partial(finish_kernel, [d.shape[2] for d in done]),
            out_shape=(
                jax.ShapeDtypeStruct(mom.shape, f32),
                jax.ShapeDtypeStruct((rows, LANES), f32),
            ),
            in_specs=[VMEM] * (5 + len(done)),
            out_specs=(VMEM, VMEM),
            scratch_shapes=[pltpu.VMEM((rows, GROUP), f32)],
            compiler_params=PARAMS,
        )(basis, basis.T, wide, wide.T, mom, *done)
    with jax.named_scope("band"):
        others = [along("rep", s, band) for s in (1, 2, 3)]
    with jax.named_scope("update"):
        (update,) = call(update_kernel, [(mom.shape, f32)], jnp.asarray(basis.T), jnp.asarray(wide.T), band, *others)
    return update[None], new[None, None]


def solution(mesh):
    fine = Mesh(mesh.devices.reshape(4, 2, 4, 4, 2), ("rep", "zh", "x", "y", "core"))
    every = ("rep", "zh", "x", "y", "core")
    return jax.shard_map(
        on_device,
        mesh=fine,
        in_specs=(
            P(None, every, None),
            P(None, every, None),
            P("rep", None, every[1:], None),
        ),
        out_specs=(P(None, every[1:], None), P("rep", None, every[1:], None)),
        check_vma=False,
    )
```
